256 devices in a mesh: dc: 32 (over z, x_hi, core), tp: 8 (over x_lo, y).
Axes of the slice: x: 4 (x_hi: 2, x_lo: 2; x = x_hi * 2 + x_lo), y: 4, z: 8, core: 2. Of those that a mesh axis runs over, the one named last changes fastest.
Arguments:
- query_rows: bfloat16 [6144, 4096], P(('dc', 'tp'))
- key_rows: bfloat16 [6144, 1024], P(('dc', 'tp'))
- value_rows: bfloat16 [6144, 1024], P(('dc', 'tp')), may hold values from -3 to 3
- grad_output: bfloat16 [6144, 4096], P(('dc', 'tp')), may hold values from -1.5 to 1.5
- span_order: int32 [64], replicated, may hold values from 0 to 63, each once
- doc_lengths: int32 [8], replicated, may hold values from 1 to 3072, 6144 in all
Outputs:
- attended: bfloat16 [6144, 4096], P(('dc', 'tp'))
- grad_query: bfloat16 [6144, 4096], P(('dc', 'tp'))
- grad_key: bfloat16 [6144, 1024], P(('dc', 'tp'))
- grad_value: bfloat16 [6144, 1024], P(('dc', 'tp'))
The draws below stay inside these ranges and needn't reach their ends.
Inputs may be any that keep to these rules, and one draw needn't show every extreme that they name: `span_order`: a permutation of the 64 blocks. `doc_lengths`: they sum to 6144, and the longest is exactly 3072.
All inputs are finite; a program needn't handle non-finite values.
Results may differ from the reference program's by a relative error of at most 0.035.
Values may be sent and summed in bfloat16 or wider, within the bound.
No kernel may reach another device: no remote copies, remote signals or barrier semaphores. Data moves between devices by JAX's collectives and lax.ppermute only.
A program may use at most 128 MiB of HBM per device.

```python
import math
import jax
import jax.numpy as jnp
import numpy as np
from jax import lax

H = 32
KVH = 8
HD = 128
NDOC = 8
SPAN = 96
NTOK = 6144
NCH = 64


def draw_query_rows(key, part):
    key = jax.random.fold_in(key, 1)
    values = jnp.clip(jax.random.normal(key, (NTOK, H * HD), jnp.float32), -5.0, 5.0)
    return values.astype(jnp.bfloat16)


def draw_key_rows(key, part):
    key = jax.random.fold_in(key, 2)
    values = jnp.clip(jax.random.normal(key, (NTOK, KVH * HD), jnp.float32), -5.0, 5.0)
    return values.astype(jnp.bfloat16)


def block_scale(rng, extent, cuts, smallest, largest):
    def one(dim, parts):
        steps = jax.random.uniform(jax.random.fold_in(jax.random.fold_in(rng, 6), dim), (parts,), jnp.float32, smallest / len(cuts), largest / len(cuts))
        return jnp.repeat(jnp.exp(steps), extent[dim] // parts).reshape((-1,) + (1,) * (len(extent) - dim - 1))

    gain = one(*cuts[0])
    for cut in cuts[1:]:
        gain = gain * one(*cut)
    return gain


def split_up(number_of, total, most, skew):
    loads = [(1 << 20) // math.isqrt(grade ** skew) + 1 for grade in range(2, number_of + 1)]
    spare, given = total - most - (number_of - 1), [1] * (number_of - 1)
    while spare > 0:
        movable = [i for i in range(number_of - 1) if given[i] < most]
        pool, budget = sum([loads[i] for i in movable]), spare
        for i in movable:
            addition = min(most - given[i], max(1, budget * loads[i] // pool), spare)
            given[i] = given[i] + addition
            spare = spare - addition
    return np.array([most] + given)


def uneven(key, amount, total, reach, skew):
    if amount == 2:
        one = jax.random.randint(key, (), max(1, total - reach), min(reach, total - 1) + 1)
        return jnp.stack([one, total - one])
    tallies = jnp.asarray(split_up(amount, total, reach, skew), jnp.int32)
    pairs = (amount - 1) // 2
    source_of, taker = tallies[1:1 + 2 * pairs:2], tallies[2:2 + 2 * pairs:2]
    room = jnp.minimum(source_of - 1, reach - taker)
    moved = jax.random.randint(jax.random.fold_in(key, 1), (pairs,), 0, 1 << 20) % (room + 1)
    tallies = tallies.at[1:1 + 2 * pairs:2].set(source_of - moved).at[2:2 + 2 * pairs:2].set(taker + moved)
    return tallies[jax.random.permutation(jax.random.fold_in(key, 2), amount)]


def noise(rng, extent, width, bound, shards=(), held_as=jnp.bfloat16):
    result = jax.random.normal(rng, extent, jnp.float32) * width
    if len(shards) > 0:
        result = block_scale(rng, extent, shards, -0.22, 0.18) * result
    return jnp.clip(result, min=-bound, max=bound).astype(held_as)


def setup_inputs(seed: int = 0) -> dict:
    arg_keys = jax.random.split(jax.random.key(seed), 7)
    query_rows = draw_query_rows(jax.random.fold_in(arg_keys[6], 71), 0)
    key_rows = draw_key_rows(jax.random.fold_in(arg_keys[6], 71), 0)
    value_rows = noise(arg_keys[2], (NTOK, KVH * HD), 0.5, 3.0, ((0, 256),))
    grad_output = noise(arg_keys[3], (NTOK, H * HD), 0.25, 1.5, ((0, 256),))
    span_order = jax.random.permutation(arg_keys[4], NCH).astype(jnp.int32)
    doc_lengths = uneven(arg_keys[5], NDOC, NTOK, NTOK // 2, 2).astype(jnp.int32)
    return {"query_rows": query_rows, "key_rows": key_rows, "value_rows": value_rows, "grad_output": grad_output, "span_order": span_order, "doc_lengths": doc_lengths}


BIG_NEG = -1.0e30


def reference(query_rows, key_rows, value_rows, grad_output, span_order, doc_lengths):
    row_ids = jnp.arange(NTOK, dtype=jnp.int32)
    places = span_order[row_ids // SPAN].astype(jnp.int32) * SPAN + row_ids % SPAN
    doc_ends = jnp.cumsum(doc_lengths)
    docs = jnp.sum((places[:, None] >= doc_ends[None, :]).astype(jnp.int32), axis=1)
    visible = (docs[:, None] == docs[None, :]) & (places[None, :] <= places[:, None])
    scale = HD ** -0.5
    group = H // KVH
    query_heads = query_rows.reshape(NTOK, H, HD).transpose(1, 0, 2)
    grad_heads = grad_output.reshape(NTOK, H, HD).transpose(1, 0, 2)
    key_heads = jnp.repeat(key_rows.reshape(NTOK, KVH, HD).transpose(1, 0, 2), group, axis=0)
    value_heads = jnp.repeat(value_rows.reshape(NTOK, KVH, HD).transpose(1, 0, 2), group, axis=0)

    def one_head(inputs_head):
        query_part, key_part, value_part, grad_part = inputs_head
        scores = jnp.dot(query_part, key_part.T, preferred_element_type=jnp.float32) * scale
        masked = jnp.where(visible, scores, BIG_NEG)
        top = jnp.max(masked, axis=1)
        weights = jnp.where(visible, jnp.exp(masked - top[:, None]), 0.0)
        total = jnp.sum(weights, axis=1)
        log_total = top + jnp.log(total)
        attended = (jnp.dot(weights.astype(jnp.bfloat16), value_part, preferred_element_type=jnp.float32) / total[:, None]).astype(jnp.bfloat16)
        grad_dot = jnp.sum(grad_part.astype(jnp.float32) * attended.astype(jnp.float32), axis=1)
        probs = jnp.exp(jnp.where(visible, scores - log_total[:, None], BIG_NEG))
        value_grad = jnp.dot(probs.astype(jnp.bfloat16).T, grad_part, preferred_element_type=jnp.float32)
        prob_grad = jnp.dot(grad_part, value_part.T, preferred_element_type=jnp.float32)
        score_grad = (probs * (prob_grad - grad_dot[:, None]) * scale).astype(jnp.bfloat16)
        query_grad = jnp.dot(score_grad, key_part, preferred_element_type=jnp.float32).astype(jnp.bfloat16)
        key_grad = jnp.dot(score_grad.T, query_part, preferred_element_type=jnp.float32)
        return attended, query_grad, key_grad, value_grad

    attended, query_grad, key_grad, value_grad = lax.map(one_head, (query_heads, key_heads, value_heads, grad_heads))
    attended = attended.transpose(1, 0, 2).reshape(NTOK, H * HD)
    query_grad = query_grad.transpose(1, 0, 2).reshape(NTOK, H * HD)
    key_grad = jnp.sum(key_grad.reshape(KVH, group, NTOK, HD), axis=1).transpose(1, 0, 2).reshape(NTOK, KVH * HD).astype(jnp.bfloat16)
    value_grad = jnp.sum(value_grad.reshape(KVH, group, NTOK, HD), axis=1).transpose(1, 0, 2).reshape(NTOK, KVH * HD).astype(jnp.bfloat16)
    return (attended, query_grad, key_grad, value_grad)
```

```python
import jax
import jax.numpy as jnp
from jax import lax
from jax.experimental import pallas as pl
from jax.experimental.pallas import tpu as pltpu
from jax.sharding import Mesh, PartitionSpec as P

HD = 128
GROUP = 4
KVH = 8
SPAN = 96
QTR = 24
NTOK = 6144
NSPAN = 64
NDOC = 8
TILE = 512
NTILE = NTOK // TILE
ROWS = 4 * QTR * GROUP
SCALE = HD**-0.5
LOG2E = 1.4426950408889634
NEG = -1e30

AXES = ("z", "xh", "c", "xl", "y")
PLANE = ("xh", "xl", "y")

NT = (((1,), (1,)), ((), ()))
NN = (((1,), (0,)), ((), ()))


def dot(a, b, dims=NN):
    return lax.dot_general(a, b, dims, preferred_element_type=jnp.float32)


def doc_start(ends, place):
    start = jnp.zeros_like(place)
    for end in ends:
        start = jnp.where(end <= place, end, start)
    return start


def attention_kernel(
    where_ref,
    order_ref,
    lens_ref,
    kv_own_ref,
    kv_other_ref,
    qg_ref,
    outs_ref,
    dkv_own_ref,
    dkv_other_ref,
    k_ref,
    v_ref,
    s_ref,
    p_ref,
    m_ref,
    acc_ref,
    dq_ref,
    dkt_ref,
    dvt_ref,
    dkv_ref,
    place_ref,
    perm_ref,
):
    xh, c, xl, y = (where_ref[i] for i in range(4))

    v_ref[:, HD:] = jnp.ones((NTOK, HD), jnp.bfloat16)

    def place_keys(z, carry):
        for ref, core in ((kv_own_ref, c), (kv_other_ref, 1 - c)):
            for x in range(4):
                span = z * 8 + (x // 2) * 4 + core * 2 + x % 2
                first = pl.multiple_of(order_ref[span] * SPAN, 32)
                rows = jnp.concatenate(
                    [ref[x * 4 + j, z].astype(jnp.float32) for j in range(4)], axis=0
                ).astype(jnp.bfloat16)
                k_ref[pl.ds(first, SPAN), :] = rows[:, :HD]
                v_ref[pl.ds(first, SPAN), :HD] = rows[:, HD:]
        return carry

    lax.fori_loop(0, 8, place_keys, 0)

    ends = []
    total_len = jnp.int32(0)
    for d in range(NDOC):
        total_len = total_len + lens_ref[d]
        ends.append(total_len)

    places = [
        order_ref[j * 8 + xh * 4 + c * 2 + xl] * SPAN + y * QTR for j in range(8)
    ]
    for i in range(8):
        rank = jnp.int32(0)
        for j in range(8):
            if j != i:
                rank = rank + (places[j] < places[i]).astype(jnp.int32)
        perm_ref[rank] = i
        place_ref[rank] = places[i]

    dkt_ref[...] = jnp.zeros_like(dkt_ref)
    dvt_ref[...] = jnp.zeros_like(dvt_ref)

    for g in range(2):
        piece_ids = [perm_ref[4 * g + i] for i in range(4)]
        piece_places = [place_ref[4 * g + i] for i in range(4)]
        low = doc_start(ends, piece_places[0])
        high = piece_places[3] + QTR
        t_low = low // TILE
        t_high = (high + TILE - 1) // TILE

        q32 = []
        g32 = []
        qpos = []
        row_ids = lax.broadcasted_iota(jnp.int32, (QTR, HD), 0)
        for i in range(4):
            for h in range(GROUP):
                q32.append(qg_ref[piece_ids[i], :, h * HD : (h + 1) * HD].astype(jnp.float32))
                g32.append(
                    qg_ref[
                        piece_ids[i], :, (GROUP + h) * HD : (GROUP + h + 1) * HD
                    ].astype(jnp.float32)
                )
                qpos.append(piece_places[i] + row_ids)
        q32 = jnp.concatenate(q32, axis=0)
        g32 = jnp.concatenate(g32, axis=0)
        qpos = jnp.concatenate(qpos, axis=0)
        qstart = doc_start(ends, qpos)
        q = q32.astype(jnp.bfloat16)
        lane = lax.broadcasted_iota(jnp.int32, (ROWS, HD), 1)

        m_ref[...] = jnp.full((ROWS, HD), NEG, jnp.float32)
        acc_ref[...] = jnp.zeros_like(acc_ref)
        dq_ref[...] = jnp.zeros_like(dq_ref)

        def score_step(t, carry):
            first = pl.multiple_of(t * TILE, TILE)
            s = dot(q, k_ref[pl.ds(first, TILE), :], NT)
            top = m_ref[...]
            for j in range(TILE // HD):
                kpos = lane + (first + j * HD)
                seen = (kpos <= qpos) & (kpos >= qstart)
                part = jnp.where(seen, s[:, j * HD : (j + 1) * HD], NEG)
                s_ref[t, :, j * HD : (j + 1) * HD] = part
                top = jnp.maximum(top, part)
            m_ref[...] = top
            return carry

        lax.fori_loop(t_low, t_high, score_step, 0)
        top = jnp.max(m_ref[...], axis=1, keepdims=True)
        m_ref[...] = jnp.broadcast_to(top, (ROWS, HD))

        def value_step(t, carry):
            first = pl.multiple_of(t * TILE, TILE)
            top = m_ref[...]
            parts = [
                jnp.exp2((s_ref[t, :, j * HD : (j + 1) * HD] - top) * (SCALE * LOG2E))
                for j in range(TILE // HD)
            ]
            p = jnp.concatenate(parts, axis=1).astype(jnp.bfloat16)
            p_ref[t] = p
            acc_ref[...] += dot(p, v_ref[pl.ds(first, TILE), :])
            return carry

        lax.fori_loop(t_low, t_high, value_step, 0)
        inv = 1.0 / acc_ref[:, HD:]
        attended = (acc_ref[:, :HD] * inv).astype(jnp.bfloat16).astype(jnp.float32)
        for i in range(4):
            for h in range(GROUP):
                at = (i * GROUP + h) * QTR
                outs_ref[piece_ids[i], :, h * HD : (h + 1) * HD] = attended[
                    at : at + QTR
                ].astype(jnp.bfloat16)
        grad_dot = jnp.sum(attended * g32, axis=1, keepdims=True) * inv
        gs32 = g32 * inv
        gs = gs32.astype(jnp.bfloat16)
        qt = q32.T.astype(jnp.bfloat16)
        gst = gs32.T.astype(jnp.bfloat16)

        def grad_step(t, carry):
            first = pl.multiple_of(t * TILE, TILE)
            k = k_ref[pl.ds(first, TILE), :]
            p = p_ref[t]
            dp = dot(gs, v_ref[pl.ds(first, TILE), :HD], NT)
            ds = jnp.concatenate(
                [
                    p[:, j * HD : (j + 1) * HD].astype(jnp.float32)
                    * (dp[:, j * HD : (j + 1) * HD] - grad_dot)
                    for j in range(TILE // HD)
                ],
                axis=1,
            ).astype(jnp.bfloat16)
            dvt_ref[:, pl.ds(first, TILE)] += dot(gst, p)
            dq_ref[...] += dot(ds, k)
            dkt_ref[:, pl.ds(first, TILE)] += dot(qt, ds)
            return carry

        lax.fori_loop(t_low, t_high, grad_step, 0)
        dq = dq_ref[...] * SCALE
        for i in range(4):
            for h in range(GROUP):
                at = (i * GROUP + h) * QTR
                outs_ref[piece_ids[i], :, (GROUP + h) * HD : (GROUP + h + 1) * HD] = dq[
                    at : at + QTR
                ].astype(jnp.bfloat16)

    def turn(t, carry):
        first = pl.multiple_of(t * TILE, TILE)
        dkv_ref[pl.ds(first, TILE), :HD] = dkt_ref[:, pl.ds(first, TILE)].T * SCALE
        dkv_ref[pl.ds(first, TILE), HD:] = dvt_ref[:, pl.ds(first, TILE)].T
        return carry

    lax.fori_loop(0, NTILE, turn, 0)

    def give_grads(z, carry):
        for ref, core in ((dkv_own_ref, c), (dkv_other_ref, 1 - c)):
            for x in range(4):
                span = z * 8 + (x // 2) * 4 + core * 2 + x % 2
                first = pl.multiple_of(order_ref[span] * SPAN, 32)
                for j in range(4):
                    ref[x * 4 + j, z] = dkv_ref[pl.ds(first + j * QTR, QTR), :].astype(jnp.bfloat16)
        return carry

    lax.fori_loop(0, 8, give_grads, 0)


def attention(where, order, lens, kv_own, kv_other, qg):
    smem = pl.BlockSpec(memory_space=pltpu.SMEM)
    vmem = pl.BlockSpec(memory_space=pltpu.VMEM)
    bf, f32 = jnp.bfloat16, jnp.float32
    return pl.pallas_call(
        attention_kernel,
        out_shape=(
            jax.ShapeDtypeStruct(qg.shape, bf),
            jax.ShapeDtypeStruct(kv_own.shape, bf),
            jax.ShapeDtypeStruct(kv_own.shape, bf),
        ),
        in_specs=[smem] * 3 + [vmem] * 3,
        out_specs=[vmem] * 3,
        scratch_shapes=[
            pltpu.VMEM((NTOK, HD), bf),
            pltpu.VMEM((NTOK, 2 * HD), bf),
            pltpu.VMEM((NTILE, ROWS, TILE), f32),
            pltpu.VMEM((NTILE, ROWS, TILE), bf),
            pltpu.VMEM((ROWS, HD), f32),
            pltpu.VMEM((ROWS, 2 * HD), f32),
            pltpu.VMEM((ROWS, HD), f32),
            pltpu.VMEM((HD, NTOK), f32),
            pltpu.VMEM((HD, NTOK), f32),
            pltpu.VMEM((NTOK, 2 * HD), f32),
            pltpu.SMEM((8,), jnp.int32),
            pltpu.SMEM((8,), jnp.int32),
        ],
        compiler_params=pltpu.CompilerParams(vmem_limit_bytes=52 * 1024 * 1024),
        cost_estimate=pl.CostEstimate(
            flops=4 * 10**9, bytes_accessed=10**7, transcendentals=2 * 10**6
        ),
    )(where, order, lens, kv_own, kv_other, qg)


def swap_cores(x):
    return lax.ppermute(x, "c", [(0, 1), (1, 0)])


def per_device(query_rows, key_rows, value_rows, grad_output, span_order, doc_lengths):
    kv = jnp.concatenate(
        [key_rows.reshape(QTR, KVH, HD), value_rows.reshape(QTR, KVH, HD)], axis=2
    ).transpose(1, 0, 2)
    kv = lax.all_to_all(kv, "z", split_axis=0, concat_axis=0, tiled=True)
    kv_own = lax.all_to_all(
        jnp.broadcast_to(kv[None], (16,) + kv.shape), PLANE, split_axis=0, concat_axis=0, tiled=True
    )
    kv_other = swap_cores(kv_own)
    qg = jnp.concatenate(
        [query_rows.reshape(QTR, KVH, -1), grad_output.reshape(QTR, KVH, -1)], axis=2
    ).transpose(1, 0, 2)
    qg = lax.all_to_all(qg, "z", split_axis=0, concat_axis=0, tiled=True)
    where = jnp.stack([lax.axis_index(a) for a in ("xh", "c", "xl", "y")]).astype(jnp.int32)
    outs, dkv_own, dkv_other = attention(where, span_order, doc_lengths, kv_own, kv_other, qg)

    dkv = (dkv_own.astype(jnp.float32) + swap_cores(dkv_other).astype(jnp.float32)).astype(
        jnp.bfloat16
    )
    dkv = lax.all_to_all(dkv, PLANE, split_axis=0, concat_axis=0, tiled=True)
    dkv = jnp.sum(dkv.astype(jnp.float32), axis=0).astype(jnp.bfloat16)
    dkv = lax.all_to_all(dkv, "z", split_axis=0, concat_axis=0, tiled=True)
    outs = lax.all_to_all(outs, "z", split_axis=0, concat_axis=0, tiled=True)
    half = GROUP * HD
    return (
        outs[:, :, :half].transpose(1, 0, 2).reshape(QTR, -1),
        outs[:, :, half:].transpose(1, 0, 2).reshape(QTR, -1),
        dkv[:, :, :HD].transpose(1, 0, 2).reshape(QTR, -1),
        dkv[:, :, HD:].transpose(1, 0, 2).reshape(QTR, -1),
    )


def solution(mesh):
    fine = Mesh(mesh.devices.reshape(8, 2, 2, 2, 4), AXES)
    rows = P(AXES, None)
    return jax.shard_map(
        per_device,
        mesh=fine,
        in_specs=(rows, rows, rows, rows, P(), P()),
        out_specs=(rows, rows, rows, rows),
        check_vma=False,
    )
```

```python
import jax
import jax.numpy as jnp
from jax import lax
from jax.experimental import pallas as pl
from jax.experimental.pallas import tpu as pltpu
from jax.sharding import Mesh, PartitionSpec as P

HD = 128
GROUP = 4
KVH = 8
SPAN = 96
QTR = 24
NTOK = 6144
NSPAN = 64
NDOC = 8
TILE = 512
NTILE = NTOK // TILE
ROWS = 4 * QTR * GROUP
SCALE = HD**-0.5
LOG2E = 1.4426950408889634
NEG = -1e30

AXES = ("z", "xh", "c", "xl", "y")
PLANE = ("xh", "c", "xl", "y")

NT = (((1,), (1,)), ((), ()))
NN = (((1,), (0,)), ((), ()))


def dot(a, b, dims=NN):
    return lax.dot_general(a, b, dims, preferred_element_type=jnp.float32)


def doc_start(ends, place):
    start = jnp.zeros_like(place)
    for end in ends:
        start = jnp.where(end <= place, end, start)
    return start


def block_rows(order_ref, core, x, y, near, far, z):
    dx = jnp.where(core == 0, far, near)
    dy = jnp.where(core == 0, near, far)
    bx, by = (x - dx) & 3, (y - dy) & 3
    span = z * 8 + (bx >> 1) * 4 + core * 2 + (bx & 1)
    return pl.multiple_of(order_ref[span] * SPAN + by * QTR, 8)


def attention_kernel(where_ref, order_ref, lens_ref, *refs):
    own_refs, other_refs, (qg_ref, outs_ref), refs = refs[:4], refs[4:8], refs[8:10], refs[10:]
    down_refs, dother_refs, refs = refs[:4], refs[4:8], refs[8:]
    (
        k_ref,
        v_ref,
        s_ref,
        p_ref,
        m_ref,
        acc_ref,
        dq_ref,
        dkt_ref,
        dvt_ref,
        dkv_ref,
        place_ref,
        perm_ref,
    ) = refs
    xh, c, xl, y = (where_ref[i] for i in range(4))
    x = xh * 2 + xl

    v_ref[:, HD:] = jnp.ones((NTOK, HD), jnp.bfloat16)

    def place_keys(z, carry):
        for group, core in ((own_refs, c), (other_refs, 1 - c)):
            for far in range(4):
                for near in range(4):
                    first = block_rows(order_ref, core, x, y, near, far, z)
                    dkv_ref[pl.ds(first, QTR), :] = group[far][near, z].astype(jnp.float32)
        return carry

    lax.fori_loop(0, 8, place_keys, 0)

    def round_keys(t, carry):
        first = pl.multiple_of(t * TILE, TILE)
        k_ref[pl.ds(first, TILE), :] = dkv_ref[pl.ds(first, TILE), :HD].astype(jnp.bfloat16)
        v_ref[pl.ds(first, TILE), :HD] = dkv_ref[pl.ds(first, TILE), HD:].astype(jnp.bfloat16)
        return carry

    lax.fori_loop(0, NTILE, round_keys, 0)

    ends = []
    total_len = jnp.int32(0)
    for d in range(NDOC):
        total_len = total_len + lens_ref[d]
        ends.append(total_len)

    places = [
        order_ref[j * 8 + xh * 4 + c * 2 + xl] * SPAN + y * QTR for j in range(8)
    ]
    for i in range(8):
        rank = jnp.int32(0)
        for j in range(8):
            if j != i:
                rank = rank + (places[j] < places[i]).astype(jnp.int32)
        perm_ref[rank] = i
        place_ref[rank] = places[i]

    dkt_ref[...] = jnp.zeros_like(dkt_ref)
    dvt_ref[...] = jnp.zeros_like(dvt_ref)

    for g in range(2):
        piece_ids = [perm_ref[4 * g + i] for i in range(4)]
        piece_places = [place_ref[4 * g + i] for i in range(4)]
        low = doc_start(ends, piece_places[0])
        high = piece_places[3] + QTR
        t_low = low // TILE
        t_high = (high + TILE - 1) // TILE

        q32 = []
        g32 = []
        qpos = []
        row_ids = lax.broadcasted_iota(jnp.int32, (QTR, HD), 0)
        for i in range(4):
            for h in range(GROUP):
                q32.append(qg_ref[piece_ids[i], :, h * HD : (h + 1) * HD].astype(jnp.float32))
                g32.append(
                    qg_ref[
                        piece_ids[i], :, (GROUP + h) * HD : (GROUP + h + 1) * HD
                    ].astype(jnp.float32)
                )
                qpos.append(piece_places[i] + row_ids)
        q32 = jnp.concatenate(q32, axis=0)
        g32 = jnp.concatenate(g32, axis=0)
        qpos = jnp.concatenate(qpos, axis=0)
        qstart = doc_start(ends, qpos)
        q = q32.astype(jnp.bfloat16)
        lane = lax.broadcasted_iota(jnp.int32, (ROWS, HD), 1)

        m_ref[...] = jnp.full((ROWS, HD), NEG, jnp.float32)
        acc_ref[...] = jnp.zeros_like(acc_ref)
        dq_ref[...] = jnp.zeros_like(dq_ref)

        def score_step(t, carry):
            first = pl.multiple_of(t * TILE, TILE)
            s = dot(q, k_ref[pl.ds(first, TILE), :], NT)
            top = m_ref[...]
            for j in range(TILE // HD):
                kpos = lane + (first + j * HD)
                seen = (kpos <= qpos) & (kpos >= qstart)
                part = jnp.where(seen, s[:, j * HD : (j + 1) * HD], NEG)
                s_ref[t, :, j * HD : (j + 1) * HD] = part
                top = jnp.maximum(top, part)
            m_ref[...] = top
            return carry

        lax.fori_loop(t_low, t_high, score_step, 0)
        top = jnp.max(m_ref[...], axis=1, keepdims=True)
        m_ref[...] = jnp.broadcast_to(top, (ROWS, HD))

        def value_step(t, carry):
            first = pl.multiple_of(t * TILE, TILE)
            top = m_ref[...]
            parts = [
                jnp.exp2((s_ref[t, :, j * HD : (j + 1) * HD] - top) * (SCALE * LOG2E))
                for j in range(TILE // HD)
            ]
            p = jnp.concatenate(parts, axis=1).astype(jnp.bfloat16)
            p_ref[t] = p
            acc_ref[...] += dot(p, v_ref[pl.ds(first, TILE), :])
            return carry

        lax.fori_loop(t_low, t_high, value_step, 0)
        inv = 1.0 / acc_ref[:, HD:]
        attended = (acc_ref[:, :HD] * inv).astype(jnp.bfloat16).astype(jnp.float32)
        for i in range(4):
            for h in range(GROUP):
                at = (i * GROUP + h) * QTR
                outs_ref[piece_ids[i], :, h * HD : (h + 1) * HD] = attended[
                    at : at + QTR
                ].astype(jnp.bfloat16)
        grad_dot = jnp.sum(attended * g32, axis=1, keepdims=True) * inv
        gs32 = g32 * inv
        gs = gs32.astype(jnp.bfloat16)
        qt = q32.T.astype(jnp.bfloat16)
        gst = gs32.T.astype(jnp.bfloat16)

        def grad_step(t, carry):
            first = pl.multiple_of(t * TILE, TILE)
            k = k_ref[pl.ds(first, TILE), :]
            p = p_ref[t]
            dp = dot(gs, v_ref[pl.ds(first, TILE), :HD], NT)
            ds = jnp.concatenate(
                [
                    p[:, j * HD : (j + 1) * HD].astype(jnp.float32)
                    * (dp[:, j * HD : (j + 1) * HD] - grad_dot)
                    for j in range(TILE // HD)
                ],
                axis=1,
            ).astype(jnp.bfloat16)
            dvt_ref[:, pl.ds(first, TILE)] += dot(gst, p)
            dq_ref[...] += dot(ds, k)
            dkt_ref[:, pl.ds(first, TILE)] += dot(qt, ds)
            return carry

        lax.fori_loop(t_low, t_high, grad_step, 0)
        dq = dq_ref[...] * SCALE
        for i in range(4):
            for h in range(GROUP):
                at = (i * GROUP + h) * QTR
                outs_ref[piece_ids[i], :, (GROUP + h) * HD : (GROUP + h + 1) * HD] = dq[
                    at : at + QTR
                ].astype(jnp.bfloat16)

    def turn(t, carry):
        first = pl.multiple_of(t * TILE, TILE)
        dkv_ref[pl.ds(first, TILE), :HD] = dkt_ref[:, pl.ds(first, TILE)].T * SCALE
        dkv_ref[pl.ds(first, TILE), HD:] = dvt_ref[:, pl.ds(first, TILE)].T
        return carry

    lax.fori_loop(0, NTILE, turn, 0)

    def give_grads(z, carry):
        for group, core in ((down_refs, c), (dother_refs, 1 - c)):
            for far in range(4):
                for near in range(4):
                    first = block_rows(order_ref, core, x, y, near, far, z)
                    group[far][near, z] = dkv_ref[pl.ds(first, QTR), :].astype(jnp.bfloat16)
        return carry

    lax.fori_loop(0, 8, give_grads, 0)


def attention(where, order, lens, own, other, qg):
    smem = pl.BlockSpec(memory_space=pltpu.SMEM)
    vmem = pl.BlockSpec(memory_space=pltpu.VMEM)
    bf, f32 = jnp.bfloat16, jnp.float32
    block = jax.ShapeDtypeStruct(own[0].shape, bf)
    outs = pl.pallas_call(
        attention_kernel,
        out_shape=(jax.ShapeDtypeStruct(qg.shape, bf),) + (block,) * 8,
        in_specs=[smem] * 3 + [vmem] * 9,
        out_specs=[vmem] * 9,
        scratch_shapes=[
            pltpu.VMEM((NTOK, HD), bf),
            pltpu.VMEM((NTOK, 2 * HD), bf),
            pltpu.VMEM((NTILE, ROWS, TILE), f32),
            pltpu.VMEM((NTILE, ROWS, TILE), bf),
            pltpu.VMEM((ROWS, HD), f32),
            pltpu.VMEM((ROWS, 2 * HD), f32),
            pltpu.VMEM((ROWS, HD), f32),
            pltpu.VMEM((HD, NTOK), f32),
            pltpu.VMEM((HD, NTOK), f32),
            pltpu.VMEM((NTOK, 2 * HD), f32),
            pltpu.SMEM((8,), jnp.int32),
            pltpu.SMEM((8,), jnp.int32),
        ],
        compiler_params=pltpu.CompilerParams(vmem_limit_bytes=52 * 1024 * 1024),
        cost_estimate=pl.CostEstimate(
            flops=4 * 10**9, bytes_accessed=10**7, transcendentals=2 * 10**6
        ),
    )(where, order, lens, *own, *other, qg)
    return outs[0], outs[1:5], outs[5:9]


def swap_cores(x):
    return lax.ppermute(x, "c", [(0, 1), (1, 0)])


def shift(x, steps, stage):
    pairs = []
    for c in range(2):
        for i in range(4):
            for y in range(4):
                if c == stage:
                    to = (i, (y + steps) % 4)
                else:
                    to = ((i + steps) % 4, y)
                at = lambda a, b: (((a // 2) * 2 + c) * 2 + a % 2) * 4 + b
                pairs.append((at(i, y), at(*to)))
    return lax.ppermute(x, PLANE, pairs)


def total(*parts):
    return sum(p.astype(jnp.float32) for p in parts).astype(jnp.bfloat16)


def per_device(query_rows, key_rows, value_rows, grad_output, span_order, doc_lengths):
    kv = jnp.concatenate(
        [key_rows.reshape(QTR, KVH, HD), value_rows.reshape(QTR, KVH, HD)], axis=2
    ).transpose(1, 0, 2)
    kv = lax.all_to_all(kv, "z", split_axis=0, concat_axis=0, tiled=True)
    qg = jnp.concatenate(
        [query_rows.reshape(QTR, KVH, -1), grad_output.reshape(QTR, KVH, -1)], axis=2
    ).transpose(1, 0, 2)
    qg = lax.all_to_all(qg, "z", split_axis=0, concat_axis=0, tiled=True)
    near = jnp.stack([kv] + [shift(kv, i, 0) for i in range(1, 4)])
    own = [near] + [shift(near, i, 1) for i in range(1, 4)]
    other = [swap_cores(b) for b in own]
    where = jnp.stack([lax.axis_index(a) for a in ("xh", "c", "xl", "y")]).astype(jnp.int32)
    outs, down, dother = attention(where, span_order, doc_lengths, own, other, qg)

    outs = lax.all_to_all(outs, "z", split_axis=0, concat_axis=0, tiled=True)
    dother = [swap_cores(b) for b in dother]
    far = [shift(total(down[i], dother[i]), 4 - i, 1) for i in range(1, 4)]
    near = total(down[0], dother[0], *far)
    dkv = total(near[0], *[shift(near[i], 4 - i, 0) for i in range(1, 4)])
    dkv = lax.all_to_all(dkv, "z", split_axis=0, concat_axis=0, tiled=True)
    half = GROUP * HD
    return (
        outs[:, :, :half].transpose(1, 0, 2).reshape(QTR, -1),
        outs[:, :, half:].transpose(1, 0, 2).reshape(QTR, -1),
        dkv[:, :, :HD].transpose(1, 0, 2).reshape(QTR, -1),
        dkv[:, :, HD:].transpose(1, 0, 2).reshape(QTR, -1),
    )


def solution(mesh):
    fine = Mesh(mesh.devices.reshape(8, 2, 2, 2, 4), AXES)
    rows = P(AXES, None)
    return jax.shard_map(
        per_device,
        mesh=fine,
        in_specs=(rows, rows, rows, rows, P(), P()),
        out_specs=(rows, rows, rows, rows),
        check_vma=False,
    )
```

```python
import jax
import jax.numpy as jnp
from jax import lax
from jax.experimental import pallas as pl
from jax.experimental.pallas import tpu as pltpu
from jax.sharding import Mesh, PartitionSpec as P

HD = 128
GROUP = 4
KVH = 8
SPAN = 96
QTR = 24
NTOK = 6144
NSPAN = 64
NDOC = 8
TILE = 1536
HALF = TILE // 2
NTILE = -(-NTOK // TILE)
PIECE = QTR * GROUP
ROWS = 8 * PIECE
LANES = 256
SCALE = HD**-0.5
LOG2E = 1.4426950408889634
NEG = -1e30

AXES = ("z", "xh", "c", "xl", "y")
PLANE = ("xh", "c", "xl", "y")

NT = (((1,), (1,)), ((), ()))
NN = (((1,), (0,)), ((), ()))


def dot(a, b, dims=NN):
    return lax.dot_general(a, b, dims, preferred_element_type=jnp.float32)


def doc_start(ends, place):
    start = jnp.zeros_like(place)
    for end in ends:
        start = jnp.where(end <= place, end, start)
    return start


def block_rows(order_ref, core, x, y, near, far, z):
    dx = jnp.where(core == 0, far, near)
    dy = jnp.where(core == 0, near, far)
    bx, by = (x - dx) & 3, (y - dy) & 3
    span = z * 8 + (bx >> 1) * 4 + core * 2 + (bx & 1)
    return pl.multiple_of(order_ref[span] * SPAN + by * QTR, 8)


def attention_kernel(where_ref, order_ref, lens_ref, *refs):
    in_refs, (qg_ref, outs_ref), refs = refs[:8], refs[8:10], refs[10:]
    out_refs, refs = refs[:8], refs[8:]
    (
        k_ref,
        v_ref,
        s_ref,
        p_ref,
        m_ref,
        acc_ref,
        dq_ref,
        dkt_ref,
        dvt_ref,
        dkv_ref,
        q_ref,
        g_ref,
        qpos_ref,
        blocks_ref,
        rows_ref,
        sems,
    ) = refs
    xh, c, xl, y = (where_ref[i] for i in range(4))
    x = xh * 2 + xl
    get_rows = pltpu.make_async_copy(qg_ref, rows_ref, sems.at[8])
    get_rows.start()
    get_blocks = [
        pltpu.make_async_copy(in_refs[i], blocks_ref.at[i], sems.at[i]) for i in range(8)
    ]
    for copy in get_blocks:
        copy.start()

    ends = []
    total_len = jnp.int32(0)
    for d in range(NDOC):
        total_len = total_len + lens_ref[d]
        ends.append(total_len)

    places = [
        order_ref[j * 8 + xh * 4 + c * 2 + xl] * SPAN + y * QTR for j in range(8)
    ]
    ranks = [sum((p < places[i]).astype(jnp.int32) for p in places) for i in range(8)]
    sorted_places = [
        sum(jnp.where(ranks[j] == i, places[j], 0) for j in range(8)) for i in range(8)
    ]

    get_rows.wait()
    row_ids = lax.broadcasted_iota(jnp.int32, (QTR, HD), 0)
    for pair in range(4):
        both = rows_ref[2 * pair * QTR : (2 * pair + 2) * QTR, :].astype(jnp.float32)
        for j in (2 * pair, 2 * pair + 1):
            qpos = places[j] + row_ids
            qstart = doc_start(ends, qpos)
            part = both[(j % 2) * QTR : (j % 2 + 1) * QTR]
            for h in range(GROUP):
                at = pl.ds(pl.multiple_of(ranks[j] * PIECE + h * QTR, 8), QTR)
                q_ref[at, :] = part[:, h * HD : (h + 1) * HD]
                g_ref[at, :] = part[:, (GROUP + h) * HD : (GROUP + h + 1) * HD]
                qpos_ref[0, at, :] = qpos
                qpos_ref[1, at, :] = qstart

    for i in range(8):
        core = 1 - c if i < 4 else c
        get_blocks[i].wait()

        def place_keys(zp, carry):
            for near in range(4):
                at = pl.multiple_of((near * 4 + zp) * 2 * QTR, 16)
                both = blocks_ref[i, pl.ds(at, 2 * QTR), :].astype(jnp.float32)
                for u in range(2):
                    first = block_rows(order_ref, core, x, y, near, i % 4, 2 * zp + u)
                    dkv_ref[pl.ds(first, QTR), :] = both[u * QTR : (u + 1) * QTR]
            return carry

        lax.fori_loop(0, 4, place_keys, 0)

    def round_keys(t, carry):
        first = pl.multiple_of(t * 512, 512)
        kv = dkv_ref[pl.ds(first, 512), :].astype(jnp.bfloat16)
        k_ref[pl.ds(first, 512), :] = kv[:, :HD]
        v_ref[pl.ds(first, 512), :HD] = kv[:, HD:]
        v_ref[pl.ds(first, 512), HD:] = jnp.ones((512, HD), jnp.bfloat16)
        dkt_ref[:, pl.ds(first, 512)] = jnp.zeros((HD, 512), jnp.float32)
        dvt_ref[:, pl.ds(first, 512)] = jnp.zeros((HD, 512), jnp.float32)
        return carry

    lax.fori_loop(0, NTOK // 512, round_keys, 0)

    lane = lax.broadcasted_iota(jnp.int32, (LANES, HD), 1)
    for g in range(ROWS // LANES):
        rows = slice(g * LANES, (g + 1) * LANES)
        low = doc_start(ends, sorted_places[g * LANES // PIECE])
        high = sorted_places[((g + 1) * LANES - 1) // PIECE] + QTR
        low = (low // HD) * HD
        halves = (high - low + HALF - 1) // HALF
        steps = halves >> 1

        def run(step):
            def whole(t, carry):
                step(t, TILE)
                return carry

            lax.fori_loop(0, steps, whole, 0)

            @pl.when(halves % 2 == 1)
            def _():
                step(steps, HALF)

        q = q_ref[rows, :].astype(jnp.bfloat16)
        m_ref[...] = jnp.full((LANES, HD), NEG, jnp.float32)
        acc_ref[...] = jnp.zeros_like(acc_ref)
        dq_ref[...] = jnp.zeros_like(dq_ref)

        def score_step(t, size):
            first = pl.multiple_of(jnp.minimum(low + t * TILE, NTOK - size), HD)
            s = dot(q, k_ref[pl.ds(first, size), :], NT)
            qpos = qpos_ref[0, rows, :]
            qstart = jnp.maximum(qpos_ref[1, rows, :], low + t * TILE)
            top = m_ref[...]
            for j in range(size // HD):
                kpos = lane + (first + j * HD)
                seen = (kpos <= qpos) & (kpos >= qstart)
                part = jnp.where(seen, s[:, j * HD : (j + 1) * HD], NEG)
                s_ref[t, :, j * HD : (j + 1) * HD] = part
                top = jnp.maximum(top, part)
            m_ref[...] = top

        run(score_step)
        top = jnp.max(m_ref[...], axis=1, keepdims=True)
        m_ref[...] = jnp.broadcast_to(top, (LANES, HD))

        def value_step(t, size):
            first = pl.multiple_of(jnp.minimum(low + t * TILE, NTOK - size), HD)
            top = m_ref[...]
            parts = [
                jnp.exp2((s_ref[t, :, j * HD : (j + 1) * HD] - top) * (SCALE * LOG2E))
                for j in range(size // HD)
            ]
            p = jnp.concatenate(parts, axis=1).astype(jnp.bfloat16)
            p_ref[t, :, :size] = p
            acc_ref[...] += dot(p, v_ref[pl.ds(first, size), :])

        run(value_step)
        inv = 1.0 / acc_ref[:, HD:]
        attended = (acc_ref[:, :HD] * inv).astype(jnp.bfloat16).astype(jnp.float32)
        gs32 = g_ref[rows, :] * inv
        gs = gs32.astype(jnp.bfloat16)
        grad_dot = jnp.broadcast_to(
            jnp.sum(attended * gs32, axis=1, keepdims=True), (LANES, HD)
        )
        qt = q_ref[rows, :].T.astype(jnp.bfloat16)
        gst = gs32.T.astype(jnp.bfloat16)

        def grad_step(t, size):
            first = pl.multiple_of(jnp.minimum(low + t * TILE, NTOK - size), HD)
            p = p_ref[t, :, :size]
            dp = dot(gs, v_ref[pl.ds(first, size), :HD], NT)
            ds = jnp.concatenate(
                [
                    p[:, j * HD : (j + 1) * HD].astype(jnp.float32)
                    * (dp[:, j * HD : (j + 1) * HD] - grad_dot)
                    for j in range(size // HD)
                ],
                axis=1,
            ).astype(jnp.bfloat16)
            dvt_ref[:, pl.ds(first, size)] += dot(gst, p)
            dq_ref[...] += dot(ds, k_ref[pl.ds(first, size), :])
            dkt_ref[:, pl.ds(first, size)] += dot(qt, ds)

        run(grad_step)
        q_ref[rows, :] = attended
        g_ref[rows, :] = dq_ref[...] * SCALE

    for pair in range(4):
        for h in range(GROUP):
            spots = [
                pl.ds(pl.multiple_of(ranks[j] * PIECE + h * QTR, 8), QTR)
                for j in (2 * pair, 2 * pair + 1)
            ]
            at = slice(2 * pair * QTR, (2 * pair + 2) * QTR)
            rows_ref[at, h * HD : (h + 1) * HD] = jnp.concatenate(
                [q_ref[spot, :] for spot in spots], axis=0
            ).astype(jnp.bfloat16)
            rows_ref[at, (GROUP + h) * HD : (GROUP + h + 1) * HD] = jnp.concatenate(
                [g_ref[spot, :] for spot in spots], axis=0
            ).astype(jnp.bfloat16)
    put_rows = pltpu.make_async_copy(rows_ref, outs_ref, sems.at[8])
    put_rows.start()

    def turn(t, carry):
        first = pl.multiple_of(t * 512, 512)
        dkv_ref[pl.ds(first, 512), :HD] = dkt_ref[:, pl.ds(first, 512)].T * SCALE
        dkv_ref[pl.ds(first, 512), HD:] = dvt_ref[:, pl.ds(first, 512)].T
        return carry

    lax.fori_loop(0, NTOK // 512, turn, 0)

    put_blocks = []
    for i in range(8):
        core = 1 - c if i < 4 else c

        def give_grads(zp, carry):
            for near in range(4):
                both = jnp.concatenate(
                    [
                        dkv_ref[
                            pl.ds(block_rows(order_ref, core, x, y, near, i % 4, 2 * zp + u), QTR),
                            :,
                        ]
                        for u in range(2)
                    ],
                    axis=0,
                )
                at = pl.multiple_of((near * 4 + zp) * 2 * QTR, 16)
                blocks_ref[i, pl.ds(at, 2 * QTR), :] = both.astype(jnp.bfloat16)
            return carry

        lax.fori_loop(0, 4, give_grads, 0)
        put_blocks.append(pltpu.make_async_copy(blocks_ref.at[i], out_refs[i], sems.at[i]))
        put_blocks[i].start()
    for copy in put_blocks:
        copy.wait()
    put_rows.wait()


def attention(where, order, lens, own, other, qg):
    smem = pl.BlockSpec(memory_space=pltpu.SMEM)
    anywhere = pl.BlockSpec(memory_space=pl.ANY)
    bf, f32 = jnp.bfloat16, jnp.float32
    flat = [b.reshape(-1, 2 * HD) for b in (*other, *own)]
    shape = own[0].shape
    block = jax.ShapeDtypeStruct(flat[0].shape, bf)
    rows = qg.reshape(-1, qg.shape[2])
    outs = pl.pallas_call(
        attention_kernel,
        out_shape=(jax.ShapeDtypeStruct(rows.shape, bf),) + (block,) * 8,
        in_specs=[smem] * 3 + [anywhere] * 9,
        out_specs=[anywhere] * 9,
        scratch_shapes=[
            pltpu.VMEM((NTOK, HD), bf),
            pltpu.VMEM((NTOK, 2 * HD), bf),
            pltpu.VMEM((NTILE, LANES, TILE), f32),
            pltpu.VMEM((NTILE, LANES, TILE), bf),
            pltpu.VMEM((LANES, HD), f32),
            pltpu.VMEM((LANES, 2 * HD), f32),
            pltpu.VMEM((LANES, HD), f32),
            pltpu.VMEM((HD, NTOK), f32),
            pltpu.VMEM((HD, NTOK), f32),
            pltpu.VMEM((NTOK, 2 * HD), f32),
            pltpu.VMEM((ROWS, HD), f32),
            pltpu.VMEM((ROWS, HD), f32),
            pltpu.VMEM((2, ROWS, HD), jnp.int32),
            pltpu.VMEM((8, NTOK // 8, 2 * HD), bf),
            pltpu.VMEM((8 * QTR, 2 * GROUP * HD), bf),
            pltpu.SemaphoreType.DMA((9,)),
        ],
        compiler_params=pltpu.CompilerParams(vmem_limit_bytes=58 * 1024 * 1024),
        cost_estimate=pl.CostEstimate(
            flops=4 * 10**9, bytes_accessed=10**7, transcendentals=2 * 10**6
        ),
    )(where, order, lens, *flat, rows)
    grads = [b.reshape(shape) for b in outs[1:]]
    return outs[0].reshape(qg.shape), grads[4:], grads[:4]


def swap_cores(x):
    return lax.ppermute(x, "c", [(0, 1), (1, 0)])


def shift(x, steps, stage):
    pairs = []
    for c in range(2):
        for i in range(4):
            for y in range(4):
                if c == stage:
                    to = (i, (y + steps) % 4)
                else:
                    to = ((i + steps) % 4, y)
                at = lambda a, b: (((a // 2) * 2 + c) * 2 + a % 2) * 4 + b
                pairs.append((at(i, y), at(*to)))
    return lax.ppermute(x, PLANE, pairs)


def total(*parts):
    return sum(p.astype(jnp.float32) for p in parts).astype(jnp.bfloat16)


def per_device(query_rows, key_rows, value_rows, grad_output, span_order, doc_lengths):
    kv = jnp.concatenate(
        [key_rows.reshape(QTR, KVH, HD), value_rows.reshape(QTR, KVH, HD)], axis=2
    ).transpose(1, 0, 2)
    kv = lax.all_to_all(kv, "z", split_axis=0, concat_axis=0, tiled=True)
    qg = jnp.concatenate(
        [query_rows.reshape(QTR, KVH, -1), grad_output.reshape(QTR, KVH, -1)], axis=2
    ).transpose(1, 0, 2)
    qg = lax.all_to_all(qg, "z", split_axis=0, concat_axis=0, tiled=True)
    near = jnp.stack([kv] + [shift(kv, i, 0) for i in range(1, 4)])
    own = [near] + [shift(near, i, 1) for i in range(1, 4)]
    other = [swap_cores(b) for b in own]
    where = jnp.stack([lax.axis_index(a) for a in ("xh", "c", "xl", "y")]).astype(jnp.int32)
    outs, down, dother = attention(where, span_order, doc_lengths, own, other, qg)

    outs = lax.all_to_all(outs, "z", split_axis=0, concat_axis=0, tiled=True)
    dother = [swap_cores(b) for b in dother]
    far = [shift(total(down[i], dother[i]), 4 - i, 1) for i in range(1, 4)]
    near = total(down[0], dother[0], *far)
    dkv = total(near[0], *[shift(near[i], 4 - i, 0) for i in range(1, 4)])
    dkv = lax.all_to_all(dkv, "z", split_axis=0, concat_axis=0, tiled=True)
    half = GROUP * HD
    return (
        outs[:, :, :half].transpose(1, 0, 2).reshape(QTR, -1),
        outs[:, :, half:].transpose(1, 0, 2).reshape(QTR, -1),
        dkv[:, :, :HD].transpose(1, 0, 2).reshape(QTR, -1),
        dkv[:, :, HD:].transpose(1, 0, 2).reshape(QTR, -1),
    )


def solution(mesh):
    fine = Mesh(mesh.devices.reshape(8, 2, 2, 2, 4), AXES)
    rows = P(AXES, None)
    return jax.shard_map(
        per_device,
        mesh=fine,
        in_specs=(rows, rows, rows, rows, P(), P()),
        out_specs=(rows, rows, rows, rows),
        check_vma=False,
    )
```

```python
import jax
import jax.numpy as jnp
from jax import lax
from jax.experimental import pallas as pl
from jax.experimental.pallas import tpu as pltpu
from jax.sharding import Mesh, PartitionSpec as P

HD = 128
GROUP = 4
KVH = 8
SPAN = 96
QTR = 24
NTOK = 6144
NSPAN = 64
NDOC = 8
TILE = 1536
HALF = TILE // 2
NTILE = -(-NTOK // TILE)
PIECE = QTR * GROUP
ROWS = 8 * PIECE
LANES = 256
NGROUP = ROWS // LANES
SCALE = HD**-0.5
LOG2E = 1.4426950408889634
NEG = -1e30

AXES = ("z", "xh", "c", "xl", "y")
PLANE = ("xh", "c", "xl", "y")

NT = (((1,), (1,)), ((), ()))
NN = (((1,), (0,)), ((), ()))


def dot(a, b, dims=NN):
    return lax.dot_general(a, b, dims, preferred_element_type=jnp.float32)


def doc_start(ends, place):
    start = jnp.zeros_like(place)
    for end in ends:
        start = jnp.where(end <= place, end, start)
    return start


def block_rows(order_ref, core, x, y, near, far, z):
    dx = jnp.where(core == 0, far, near)
    dy = jnp.where(core == 0, near, far)
    bx, by = (x - dx) & 3, (y - dy) & 3
    span = z * 8 + (bx >> 1) * 4 + core * 2 + (bx & 1)
    return pl.multiple_of(order_ref[span] * SPAN + by * QTR, 8)


def attention_kernel(where_ref, order_ref, lens_ref, *refs):
    in_refs, (qg_ref, outs_ref), refs = refs[:8], refs[8:10], refs[10:]
    out_refs, refs = refs[:8], refs[8:]
    (
        k_ref,
        v_ref,
        s_ref,
        p_ref,
        m_ref,
        acc_ref,
        dq_ref,
        turned_ref,
        dkt_ref,
        dvt_ref,
        dkv_ref,
        q_ref,
        g_ref,
        qpos_ref,
        blocks_ref,
        rows_ref,
        sems,
    ) = refs
    xh, c, xl, y = (where_ref[i] for i in range(4))
    x = xh * 2 + xl
    get_rows = pltpu.make_async_copy(qg_ref, rows_ref, sems.at[8])
    get_rows.start()
    get_blocks = [
        pltpu.make_async_copy(in_refs[i], blocks_ref.at[i], sems.at[i]) for i in range(8)
    ]
    for copy in get_blocks:
        copy.start()

    ends = []
    total_len = jnp.int32(0)
    for d in range(NDOC):
        total_len = total_len + lens_ref[d]
        ends.append(total_len)

    places = [
        order_ref[j * 8 + xh * 4 + c * 2 + xl] * SPAN + y * QTR for j in range(8)
    ]
    ranks = [sum((p < places[i]).astype(jnp.int32) for p in places) for i in range(8)]
    sorted_places = [
        sum(jnp.where(ranks[j] == i, places[j], 0) for j in range(8)) for i in range(8)
    ]

    get_rows.wait()
    row_ids = lax.broadcasted_iota(jnp.int32, (QTR, HD), 0)
    for pair in range(4):
        both = rows_ref[2 * pair * QTR : (2 * pair + 2) * QTR, :].astype(jnp.float32)
        for j in (2 * pair, 2 * pair + 1):
            qpos = places[j] + row_ids
            qstart = doc_start(ends, qpos)
            part = both[(j % 2) * QTR : (j % 2 + 1) * QTR]
            for h in range(GROUP):
                at = pl.ds(pl.multiple_of(ranks[j] * PIECE + h * QTR, 8), QTR)
                q_ref[at, :] = part[:, h * HD : (h + 1) * HD]
                g_ref[at, :] = part[:, (GROUP + h) * HD : (GROUP + h + 1) * HD]
                qpos_ref[0, at, :] = qpos
                qpos_ref[1, at, :] = qstart

    for i in range(8):
        core = 1 - c if i < 4 else c
        get_blocks[i].wait()

        def place_keys(zp, carry):
            for near in range(4):
                at = pl.multiple_of((near * 4 + zp) * 2 * QTR, 16)
                both = blocks_ref[i, pl.ds(at, 2 * QTR), :].astype(jnp.float32)
                for u in range(2):
                    first = block_rows(order_ref, core, x, y, near, i % 4, 2 * zp + u)
                    dkv_ref[pl.ds(first, QTR), :] = both[u * QTR : (u + 1) * QTR]
            return carry

        lax.fori_loop(0, 4, place_keys, 0)

    def round_keys(t, carry):
        first = pl.multiple_of(t * 512, 512)
        kv = dkv_ref[pl.ds(first, 512), :].astype(jnp.bfloat16)
        k_ref[pl.ds(first, 512), :] = kv[:, :HD]
        v_ref[pl.ds(first, 512), :HD] = kv[:, HD:]
        v_ref[pl.ds(first, 512), HD:] = jnp.ones((512, HD), jnp.bfloat16)
        dkt_ref[:, pl.ds(first, 512)] = jnp.zeros((HD, 512), jnp.float32)
        dvt_ref[:, pl.ds(first, 512)] = jnp.zeros((HD, 512), jnp.float32)
        return carry

    lax.fori_loop(0, NTOK // 512, round_keys, 0)

    lane = lax.broadcasted_iota(jnp.int32, (LANES, HD), 1)
    groups = []
    for g in range(ROWS // LANES):
        low = doc_start(ends, sorted_places[g * LANES // PIECE])
        high = sorted_places[((g + 1) * LANES - 1) // PIECE] + QTR
        low = (low // HD) * HD
        groups.append((g, slice(g * LANES, (g + 1) * LANES), low, (high - low + HALF - 1) // HALF))
    m_ref[...] = jnp.full(m_ref.shape, NEG, jnp.float32)
    acc_ref[...] = jnp.zeros_like(acc_ref)
    dq_ref[...] = jnp.zeros_like(dq_ref)

    def run(step, halves):
        def whole(t, carry):
            step(t, TILE)
            return carry

        lax.fori_loop(0, halves >> 1, whole, 0)

        @pl.when(halves % 2 == 1)
        def _():
            step(halves >> 1, HALF)

    for g, rows, low, halves in groups:
        q = q_ref[rows, :].astype(jnp.bfloat16)

        def score_step(t, size):
            first = pl.multiple_of(jnp.minimum(low + t * TILE, NTOK - size), HD)
            s = dot(q, k_ref[pl.ds(first, size), :], NT)
            qpos = qpos_ref[0, rows, :]
            qstart = jnp.maximum(qpos_ref[1, rows, :], low + t * TILE)
            top = m_ref[g]
            for j in range(size // HD):
                kpos = lane + (first + j * HD)
                seen = (kpos <= qpos) & (kpos >= qstart)
                part = jnp.where(seen, s[:, j * HD : (j + 1) * HD], NEG)
                s_ref[g, t, :, j * HD : (j + 1) * HD] = part
                top = jnp.maximum(top, part)
            m_ref[g] = top

        run(score_step, halves)

    m_ref[...] = jnp.broadcast_to(jnp.max(m_ref[...], axis=2, keepdims=True), m_ref.shape)

    for g, rows, low, halves in groups:

        def value_step(t, size):
            first = pl.multiple_of(jnp.minimum(low + t * TILE, NTOK - size), HD)
            top = m_ref[g]
            parts = [
                jnp.exp2((s_ref[g, t, :, j * HD : (j + 1) * HD] - top) * (SCALE * LOG2E))
                for j in range(size // HD)
            ]
            p = jnp.concatenate(parts, axis=1).astype(jnp.bfloat16)
            p_ref[g, t, :, :size] = p
            acc_ref[g] += dot(p, v_ref[pl.ds(first, size), :])

        run(value_step, halves)

    for g, rows, low, halves in groups:
        inv = 1.0 / acc_ref[g, :, HD:]
        attended = (acc_ref[g, :, :HD] * inv).astype(jnp.bfloat16).astype(jnp.float32)
        gs32 = g_ref[rows, :] * inv
        g_ref[rows, :] = gs32
        m_ref[g] = jnp.broadcast_to(
            jnp.sum(attended * gs32, axis=1, keepdims=True), (LANES, HD)
        )
        turned_ref[0, :, rows] = q_ref[rows, :].T.astype(jnp.bfloat16)
        turned_ref[1, :, rows] = gs32.T.astype(jnp.bfloat16)
        q_ref[rows, :] = attended

    for g, rows, low, halves in groups:
        gs = g_ref[rows, :].astype(jnp.bfloat16)
        qt, gst = turned_ref[0, :, rows], turned_ref[1, :, rows]
        grad_dot = m_ref[g]

        def grad_step(t, size):
            first = pl.multiple_of(jnp.minimum(low + t * TILE, NTOK - size), HD)
            p = p_ref[g, t, :, :size]
            dp = dot(gs, v_ref[pl.ds(first, size), :HD], NT)
            ds = jnp.concatenate(
                [
                    p[:, j * HD : (j + 1) * HD].astype(jnp.float32)
                    * (dp[:, j * HD : (j + 1) * HD] - grad_dot)
                    for j in range(size // HD)
                ],
                axis=1,
            ).astype(jnp.bfloat16)
            dvt_ref[:, pl.ds(first, size)] += dot(gst, p)
            dq_ref[g] += dot(ds, k_ref[pl.ds(first, size), :])
            dkt_ref[:, pl.ds(first, size)] += dot(qt, ds)

        run(grad_step, halves)

    for g, rows, low, halves in groups:
        g_ref[rows, :] = dq_ref[g] * SCALE

    for pair in range(4):
        for h in range(GROUP):
            spots = [
                pl.ds(pl.multiple_of(ranks[j] * PIECE + h * QTR, 8), QTR)
                for j in (2 * pair, 2 * pair + 1)
            ]
            at = slice(2 * pair * QTR, (2 * pair + 2) * QTR)
            rows_ref[at, h * HD : (h + 1) * HD] = jnp.concatenate(
                [q_ref[spot, :] for spot in spots], axis=0
            ).astype(jnp.bfloat16)
            rows_ref[at, (GROUP + h) * HD : (GROUP + h + 1) * HD] = jnp.concatenate(
                [g_ref[spot, :] for spot in spots], axis=0
            ).astype(jnp.bfloat16)
    put_rows = pltpu.make_async_copy(rows_ref, outs_ref, sems.at[8])
    put_rows.start()

    def turn(t, carry):
        first = pl.multiple_of(t * 2048, 2048)
        for ref, at, scale in ((dkt_ref, 0, SCALE), (dvt_ref, HD, 1.0)):
            part = ref[:, pl.ds(first, 2048)] * scale
            part = part.astype(jnp.bfloat16).T.astype(jnp.float32)
            dkv_ref[pl.ds(first, 2048), at : at + HD] = part
        return carry

    lax.fori_loop(0, NTOK // 2048, turn, 0)

    put_blocks = []
    for i in range(8):
        core = 1 - c if i < 4 else c

        def give_grads(zp, carry):
            for near in range(4):
                both = jnp.concatenate(
                    [
                        dkv_ref[
                            pl.ds(block_rows(order_ref, core, x, y, near, i % 4, 2 * zp + u), QTR),
                            :,
                        ]
                        for u in range(2)
                    ],
                    axis=0,
                )
                at = pl.multiple_of((near * 4 + zp) * 2 * QTR, 16)
                blocks_ref[i, pl.ds(at, 2 * QTR), :] = both.astype(jnp.bfloat16)
            return carry

        lax.fori_loop(0, 4, give_grads, 0)
        put_blocks.append(pltpu.make_async_copy(blocks_ref.at[i], out_refs[i], sems.at[i]))
        put_blocks[i].start()
    for copy in put_blocks:
        copy.wait()
    put_rows.wait()


def attention(where, order, lens, own, other, qg):
    smem = pl.BlockSpec(memory_space=pltpu.SMEM)
    anywhere = pl.BlockSpec(memory_space=pl.ANY)
    bf, f32 = jnp.bfloat16, jnp.float32
    flat = [b.reshape(-1, 2 * HD) for b in (*other, *own)]
    shape = own[0].shape
    block = jax.ShapeDtypeStruct(flat[0].shape, bf)
    rows = qg.reshape(-1, qg.shape[2])
    outs = pl.pallas_call(
        attention_kernel,
        out_shape=(jax.ShapeDtypeStruct(rows.shape, bf),) + (block,) * 8,
        in_specs=[smem] * 3 + [anywhere] * 9,
        out_specs=[anywhere] * 9,
        scratch_shapes=[
            pltpu.VMEM((NTOK, HD), bf),
            pltpu.VMEM((NTOK, 2 * HD), bf),
            pltpu.VMEM((NGROUP, NTILE, LANES, TILE), f32),
            pltpu.VMEM((NGROUP, NTILE, LANES, TILE), bf),
            pltpu.VMEM((NGROUP, LANES, HD), f32),
            pltpu.VMEM((NGROUP, LANES, 2 * HD), f32),
            pltpu.VMEM((NGROUP, LANES, HD), f32),
            pltpu.VMEM((2, HD, ROWS), bf),
            pltpu.VMEM((HD, NTOK), f32),
            pltpu.VMEM((HD, NTOK), f32),
            pltpu.VMEM((NTOK, 2 * HD), f32),
            pltpu.VMEM((ROWS, HD), f32),
            pltpu.VMEM((ROWS, HD), f32),
            pltpu.VMEM((2, ROWS, HD), jnp.int32),
            pltpu.VMEM((8, NTOK // 8, 2 * HD), bf),
            pltpu.VMEM((8 * QTR, 2 * GROUP * HD), bf),
            pltpu.SemaphoreType.DMA((9,)),
        ],
        compiler_params=pltpu.CompilerParams(vmem_limit_bytes=58 * 1024 * 1024),
        cost_estimate=pl.CostEstimate(
            flops=4 * 10**9, bytes_accessed=10**7, transcendentals=2 * 10**6
        ),
    )(where, order, lens, *flat, rows)
    grads = [b.reshape(shape) for b in outs[1:]]
    return outs[0].reshape(qg.shape), grads[4:], grads[:4]


def swap_cores(x):
    return lax.ppermute(x, "c", [(0, 1), (1, 0)])


def shift(x, steps, stage):
    pairs = []
    for c in range(2):
        for i in range(4):
            for y in range(4):
                if c == stage:
                    to = (i, (y + steps) % 4)
                else:
                    to = ((i + steps) % 4, y)
                at = lambda a, b: (((a // 2) * 2 + c) * 2 + a % 2) * 4 + b
                pairs.append((at(i, y), at(*to)))
    return lax.ppermute(x, PLANE, pairs)


def total(*parts):
    return sum(p.astype(jnp.float32) for p in parts).astype(jnp.bfloat16)


def per_device(query_rows, key_rows, value_rows, grad_output, span_order, doc_lengths):
    kv = jnp.concatenate(
        [key_rows.reshape(QTR, KVH, HD), value_rows.reshape(QTR, KVH, HD)], axis=2
    ).transpose(1, 0, 2)
    kv = lax.all_to_all(kv, "z", split_axis=0, concat_axis=0, tiled=True)
    qg = jnp.concatenate(
        [query_rows.reshape(QTR, KVH, -1), grad_output.reshape(QTR, KVH, -1)], axis=2
    ).transpose(1, 0, 2)
    qg = lax.all_to_all(qg, "z", split_axis=0, concat_axis=0, tiled=True)
    near = jnp.stack([kv] + [shift(kv, i, 0) for i in range(1, 4)])
    own = [near] + [shift(near, i, 1) for i in range(1, 4)]
    other = [swap_cores(b) for b in own]
    where = jnp.stack([lax.axis_index(a) for a in ("xh", "c", "xl", "y")]).astype(jnp.int32)
    outs, down, dother = attention(where, span_order, doc_lengths, own, other, qg)

    outs = lax.all_to_all(outs, "z", split_axis=0, concat_axis=0, tiled=True)
    dother = [swap_cores(b) for b in dother]
    far = [shift(total(down[i], dother[i]), 4 - i, 1) for i in range(1, 4)]
    near = total(down[0], dother[0], *far)
    dkv = total(near[0], *[shift(near[i], 4 - i, 0) for i in range(1, 4)])
    dkv = lax.all_to_all(dkv, "z", split_axis=0, concat_axis=0, tiled=True)
    half = GROUP * HD
    return (
        outs[:, :, :half].transpose(1, 0, 2).reshape(QTR, -1),
        outs[:, :, half:].transpose(1, 0, 2).reshape(QTR, -1),
        dkv[:, :, :HD].transpose(1, 0, 2).reshape(QTR, -1),
        dkv[:, :, HD:].transpose(1, 0, 2).reshape(QTR, -1),
    )


def solution(mesh):
    fine = Mesh(mesh.devices.reshape(8, 2, 2, 2, 4), AXES)
    rows = P(AXES, None)
    return jax.shard_map(
        per_device,
        mesh=fine,
        in_specs=(rows, rows, rows, rows, P(), P()),
        out_specs=(rows, rows, rows, rows),
        check_vma=False,
    )
```

```python
import jax
import jax.numpy as jnp
from jax import lax
from jax.experimental import pallas as pl
from jax.experimental.pallas import tpu as pltpu
from jax.sharding import Mesh, PartitionSpec as P

HD = 128
GROUP = 4
KVH = 8
SPAN = 96
QTR = 24
NTOK = 6144
NSPAN = 64
NDOC = 8
TILE = 1536
HALF = TILE // 2
NTILE = -(-NTOK // TILE)
PIECE = QTR * GROUP
ROWS = 8 * PIECE
LANES = 256
NGROUP = ROWS // LANES
SCALE = HD**-0.5
LOG2E = 1.4426950408889634
NEG = -1e30

AXES = ("z", "xh", "c", "xl", "y")
PLANE = ("xh", "c", "xl", "y")

NT = (((1,), (1,)), ((), ()))
NN = (((1,), (0,)), ((), ()))


def dot(a, b, dims=NN):
    return lax.dot_general(a, b, dims, preferred_element_type=jnp.float32)


def doc_start(ends, place):
    start = jnp.zeros_like(place)
    for end in ends:
        start = jnp.where(end <= place, end, start)
    return start


def block_rows(order_ref, core, x, y, near, far, z):
    dx = jnp.where(core == 0, far, near)
    dy = jnp.where(core == 0, near, far)
    bx, by = (x - dx) & 3, (y - dy) & 3
    span = z * 8 + (bx >> 1) * 4 + core * 2 + (bx & 1)
    return pl.multiple_of(order_ref[span] * SPAN + by * QTR, 8)


def attention_kernel(where_ref, order_ref, lens_ref, *refs):
    in_refs, (qg_ref, outs_ref), refs = refs[:8], refs[8:10], refs[10:]
    out_refs, refs = refs[:8], refs[8:]
    (
        k_ref,
        v_ref,
        s_ref,
        p_ref,
        m_ref,
        acc_ref,
        dq_ref,
        turned_ref,
        dkt_ref,
        dvt_ref,
        dkv_ref,
        q_ref,
        g_ref,
        qpos_ref,
        blocks_ref,
        rows_ref,
        sems,
    ) = refs
    xh, c, xl, y = (where_ref[i] for i in range(4))
    x = xh * 2 + xl
    get_rows = pltpu.make_async_copy(qg_ref, rows_ref, sems.at[8])
    get_rows.start()
    get_blocks = [
        pltpu.make_async_copy(in_refs[i], blocks_ref.at[i], sems.at[i]) for i in range(8)
    ]
    for copy in get_blocks:
        copy.start()

    ends = []
    total_len = jnp.int32(0)
    for d in range(NDOC):
        total_len = total_len + lens_ref[d]
        ends.append(total_len)

    places = [
        order_ref[j * 8 + xh * 4 + c * 2 + xl] * SPAN + y * QTR for j in range(8)
    ]
    ranks = [sum((p < places[i]).astype(jnp.int32) for p in places) for i in range(8)]
    sorted_places = [
        sum(jnp.where(ranks[j] == i, places[j], 0) for j in range(8)) for i in range(8)
    ]

    get_rows.wait()
    row_ids = lax.broadcasted_iota(jnp.int32, (QTR, HD), 0)
    for pair in range(4):
        both = rows_ref[2 * pair * QTR : (2 * pair + 2) * QTR, :].astype(jnp.float32)
        for j in (2 * pair, 2 * pair + 1):
            qpos = places[j] + row_ids
            qstart = doc_start(ends, qpos)
            part = both[(j % 2) * QTR : (j % 2 + 1) * QTR]
            for h in range(GROUP):
                at = pl.ds(pl.multiple_of(ranks[j] * PIECE + h * QTR, 8), QTR)
                q_ref[at, :] = part[:, h * HD : (h + 1) * HD]
                g_ref[at, :] = part[:, (GROUP + h) * HD : (GROUP + h + 1) * HD]
                qpos_ref[0, at, :] = qpos
                qpos_ref[1, at, :] = qstart

    for i in range(8):
        core = 1 - c if i < 4 else c
        get_blocks[i].wait()

        def place_keys(zp, carry):
            for near in range(4):
                at = pl.multiple_of((near * 4 + zp) * 2 * QTR, 16)
                both = blocks_ref[i, pl.ds(at, 2 * QTR), :].astype(jnp.float32)
                for u in range(2):
                    first = block_rows(order_ref, core, x, y, near, i % 4, 2 * zp + u)
                    dkv_ref[pl.ds(first, QTR), :] = both[u * QTR : (u + 1) * QTR]
            return carry

        lax.fori_loop(0, 4, place_keys, 0, unroll=True)

    def round_keys(t, carry):
        first = pl.multiple_of(t * 512, 512)
        kv = dkv_ref[pl.ds(first, 512), :].astype(jnp.bfloat16)
        k_ref[pl.ds(first, 512), :] = kv[:, :HD]
        v_ref[pl.ds(first, 512), :HD] = kv[:, HD:]
        v_ref[pl.ds(first, 512), HD:] = jnp.ones((512, HD), jnp.bfloat16)
        dkt_ref[:, pl.ds(first, 512)] = jnp.zeros((HD, 512), jnp.float32)
        dvt_ref[:, pl.ds(first, 512)] = jnp.zeros((HD, 512), jnp.float32)
        return carry

    lax.fori_loop(0, NTOK // 512, round_keys, 0)

    lane = lax.broadcasted_iota(jnp.int32, (LANES, HD), 1)
    groups = []
    for g in range(ROWS // LANES):
        low = doc_start(ends, sorted_places[g * LANES // PIECE])
        high = sorted_places[((g + 1) * LANES - 1) // PIECE] + QTR
        low = (low // HD) * HD
        groups.append((g, slice(g * LANES, (g + 1) * LANES), low, (high - low + HALF - 1) // HALF))
    m_ref[...] = jnp.full(m_ref.shape, NEG, jnp.float32)
    acc_ref[...] = jnp.zeros_like(acc_ref)
    dq_ref[...] = jnp.zeros_like(dq_ref)

    def run(step, halves):
        def whole(t, carry):
            step(t, TILE)
            return carry

        lax.fori_loop(0, halves >> 1, whole, 0)

        @pl.when(halves % 2 == 1)
        def _():
            step(halves >> 1, HALF)

    for g, rows, low, halves in groups:
        q = q_ref[rows, :].astype(jnp.bfloat16)

        def score_step(t, size):
            first = pl.multiple_of(jnp.minimum(low + t * TILE, NTOK - size), HD)
            s = dot(q, k_ref[pl.ds(first, size), :], NT)
            qpos = qpos_ref[0, rows, :]
            qstart = jnp.maximum(qpos_ref[1, rows, :], low + t * TILE)
            top = m_ref[g]
            for j in range(size // HD):
                kpos = lane + (first + j * HD)
                seen = (kpos <= qpos) & (kpos >= qstart)
                part = jnp.where(seen, s[:, j * HD : (j + 1) * HD], NEG)
                s_ref[g, t, :, j * HD : (j + 1) * HD] = part
                top = jnp.maximum(top, part)
            m_ref[g] = top

        run(score_step, halves)

    m_ref[...] = jnp.broadcast_to(jnp.max(m_ref[...], axis=2, keepdims=True), m_ref.shape)

    for g, rows, low, halves in groups:

        def value_step(t, size):
            first = pl.multiple_of(jnp.minimum(low + t * TILE, NTOK - size), HD)
            top = m_ref[g]
            parts = [
                jnp.exp2((s_ref[g, t, :, j * HD : (j + 1) * HD] - top) * (SCALE * LOG2E))
                for j in range(size // HD)
            ]
            p = jnp.concatenate(parts, axis=1).astype(jnp.bfloat16)
            p_ref[g, t, :, :size] = p
            acc_ref[g] += dot(p, v_ref[pl.ds(first, size), :])

        run(value_step, halves)

    for g, rows, low, halves in groups:
        inv = 1.0 / acc_ref[g, :, HD:]
        attended = (acc_ref[g, :, :HD] * inv).astype(jnp.bfloat16).astype(jnp.float32)
        gs32 = g_ref[rows, :] * inv
        g_ref[rows, :] = gs32
        m_ref[g] = jnp.broadcast_to(
            jnp.sum(attended * gs32, axis=1, keepdims=True), (LANES, HD)
        )
        turned_ref[0, :, rows] = q_ref[rows, :].T.astype(jnp.bfloat16)
        turned_ref[1, :, rows] = gs32.T.astype(jnp.bfloat16)
        q_ref[rows, :] = attended

    for g, rows, low, halves in groups:
        gs = g_ref[rows, :].astype(jnp.bfloat16)
        qt, gst = turned_ref[0, :, rows], turned_ref[1, :, rows]
        grad_dot = m_ref[g]

        def grad_step(t, size):
            first = pl.multiple_of(jnp.minimum(low + t * TILE, NTOK - size), HD)
            p = p_ref[g, t, :, :size]
            dp = dot(gs, v_ref[pl.ds(first, size), :HD], NT)
            ds = jnp.concatenate(
                [
                    p[:, j * HD : (j + 1) * HD].astype(jnp.float32)
                    * (dp[:, j * HD : (j + 1) * HD] - grad_dot)
                    for j in range(size // HD)
                ],
                axis=1,
            ).astype(jnp.bfloat16)
            dvt_ref[:, pl.ds(first, size)] += dot(gst, p)
            dq_ref[g] += dot(ds, k_ref[pl.ds(first, size), :])
            dkt_ref[:, pl.ds(first, size)] += dot(qt, ds)

        run(grad_step, halves)

    for g, rows, low, halves in groups:
        g_ref[rows, :] = dq_ref[g] * SCALE

    for pair in range(4):
        for h in range(GROUP):
            spots = [
                pl.ds(pl.multiple_of(ranks[j] * PIECE + h * QTR, 8), QTR)
                for j in (2 * pair, 2 * pair + 1)
            ]
            at = slice(2 * pair * QTR, (2 * pair + 2) * QTR)
            rows_ref[at, h * HD : (h + 1) * HD] = jnp.concatenate(
                [q_ref[spot, :] for spot in spots], axis=0
            ).astype(jnp.bfloat16)
            rows_ref[at, (GROUP + h) * HD : (GROUP + h + 1) * HD] = jnp.concatenate(
                [g_ref[spot, :] for spot in spots], axis=0
            ).astype(jnp.bfloat16)
    put_rows = pltpu.make_async_copy(rows_ref, outs_ref, sems.at[8])
    put_rows.start()

    def turn(t, carry):
        first = pl.multiple_of(t * 2048, 2048)
        for ref, at, scale in ((dkt_ref, 0, SCALE), (dvt_ref, HD, 1.0)):
            part = ref[:, pl.ds(first, 2048)] * scale
            part = part.astype(jnp.bfloat16).T.astype(jnp.float32)
            dkv_ref[pl.ds(first, 2048), at : at + HD] = part
        return carry

    lax.fori_loop(0, NTOK // 2048, turn, 0)

    put_blocks = []
    for i in range(8):
        core = 1 - c if i < 4 else c

        def give_grads(zp, carry):
            for near in range(4):
                both = jnp.concatenate(
                    [
                        dkv_ref[
                            pl.ds(block_rows(order_ref, core, x, y, near, i % 4, 2 * zp + u), QTR),
                            :,
                        ]
                        for u in range(2)
                    ],
                    axis=0,
                )
                at = pl.multiple_of((near * 4 + zp) * 2 * QTR, 16)
                blocks_ref[i, pl.ds(at, 2 * QTR), :] = both.astype(jnp.bfloat16)
            return carry

        lax.fori_loop(0, 4, give_grads, 0, unroll=True)
        put_blocks.append(pltpu.make_async_copy(blocks_ref.at[i], out_refs[i], sems.at[i]))
        put_blocks[i].start()
    for copy in put_blocks:
        copy.wait()
    put_rows.wait()


def attention(where, order, lens, own, other, qg):
    smem = pl.BlockSpec(memory_space=pltpu.SMEM)
    anywhere = pl.BlockSpec(memory_space=pl.ANY)
    bf, f32 = jnp.bfloat16, jnp.float32
    flat = [b.reshape(-1, 2 * HD) for b in (*other, *own)]
    shape = own[0].shape
    block = jax.ShapeDtypeStruct(flat[0].shape, bf)
    rows = qg.reshape(-1, qg.shape[2])
    outs = pl.pallas_call(
        attention_kernel,
        out_shape=(jax.ShapeDtypeStruct(rows.shape, bf),) + (block,) * 8,
        in_specs=[smem] * 3 + [anywhere] * 9,
        out_specs=[anywhere] * 9,
        scratch_shapes=[
            pltpu.VMEM((NTOK, HD), bf),
            pltpu.VMEM((NTOK, 2 * HD), bf),
            pltpu.VMEM((NGROUP, NTILE, LANES, TILE), f32),
            pltpu.VMEM((NGROUP, NTILE, LANES, TILE), bf),
            pltpu.VMEM((NGROUP, LANES, HD), f32),
            pltpu.VMEM((NGROUP, LANES, 2 * HD), f32),
            pltpu.VMEM((NGROUP, LANES, HD), f32),
            pltpu.VMEM((2, HD, ROWS), bf),
            pltpu.VMEM((HD, NTOK), f32),
            pltpu.VMEM((HD, NTOK), f32),
            pltpu.VMEM((NTOK, 2 * HD), f32),
            pltpu.VMEM((ROWS, HD), f32),
            pltpu.VMEM((ROWS, HD), f32),
            pltpu.VMEM((2, ROWS, HD), jnp.int32),
            pltpu.VMEM((8, NTOK // 8, 2 * HD), bf),
            pltpu.VMEM((8 * QTR, 2 * GROUP * HD), bf),
            pltpu.SemaphoreType.DMA((9,)),
        ],
        compiler_params=pltpu.CompilerParams(vmem_limit_bytes=58 * 1024 * 1024),
        cost_estimate=pl.CostEstimate(
            flops=4 * 10**9, bytes_accessed=10**7, transcendentals=2 * 10**6
        ),
    )(where, order, lens, *flat, rows)
    grads = [b.reshape(shape) for b in outs[1:]]
    return outs[0].reshape(qg.shape), grads[4:], grads[:4]


def swap_cores(x):
    return lax.ppermute(x, "c", [(0, 1), (1, 0)])


def shift(x, steps, stage):
    pairs = []
    for c in range(2):
        for i in range(4):
            for y in range(4):
                if c == stage:
                    to = (i, (y + steps) % 4)
                else:
                    to = ((i + steps) % 4, y)
                at = lambda a, b: (((a // 2) * 2 + c) * 2 + a % 2) * 4 + b
                pairs.append((at(i, y), at(*to)))
    return lax.ppermute(x, PLANE, pairs)


def total(*parts):
    return sum(p.astype(jnp.float32) for p in parts).astype(jnp.bfloat16)


def per_device(query_rows, key_rows, value_rows, grad_output, span_order, doc_lengths):
    kv = jnp.concatenate(
        [key_rows.reshape(QTR, KVH, HD), value_rows.reshape(QTR, KVH, HD)], axis=2
    ).transpose(1, 0, 2)
    kv = lax.all_to_all(kv, "z", split_axis=0, concat_axis=0, tiled=True)
    qg = jnp.concatenate(
        [query_rows.reshape(QTR, KVH, -1), grad_output.reshape(QTR, KVH, -1)], axis=2
    ).transpose(1, 0, 2)
    qg = lax.all_to_all(qg, "z", split_axis=0, concat_axis=0, tiled=True)
    near = jnp.stack([kv] + [shift(kv, i, 0) for i in range(1, 4)])
    own = [near] + [shift(near, i, 1) for i in range(1, 4)]
    other = [swap_cores(b) for b in own]
    where = jnp.stack([lax.axis_index(a) for a in ("xh", "c", "xl", "y")]).astype(jnp.int32)
    outs, down, dother = attention(where, span_order, doc_lengths, own, other, qg)

    outs = lax.all_to_all(outs, "z", split_axis=0, concat_axis=0, tiled=True)
    dother = [swap_cores(b) for b in dother]
    far = [shift(total(down[i], dother[i]), 4 - i, 1) for i in range(1, 4)]
    near = total(down[0], dother[0], *far)
    dkv = total(near[0], *[shift(near[i], 4 - i, 0) for i in range(1, 4)])
    dkv = lax.all_to_all(dkv, "z", split_axis=0, concat_axis=0, tiled=True)
    half = GROUP * HD
    return (
        outs[:, :, :half].transpose(1, 0, 2).reshape(QTR, -1),
        outs[:, :, half:].transpose(1, 0, 2).reshape(QTR, -1),
        dkv[:, :, :HD].transpose(1, 0, 2).reshape(QTR, -1),
        dkv[:, :, HD:].transpose(1, 0, 2).reshape(QTR, -1),
    )


def solution(mesh):
    fine = Mesh(mesh.devices.reshape(8, 2, 2, 2, 4), AXES)
    rows = P(AXES, None)
    return jax.shard_map(
        per_device,
        mesh=fine,
        in_specs=(rows, rows, rows, rows, P(), P()),
        out_specs=(rows, rows, rows, rows),
        check_vma=False,
    )
```

```python
import jax
import jax.numpy as jnp
from jax import lax
from jax.experimental import pallas as pl
from jax.experimental.pallas import tpu as pltpu
from jax.sharding import Mesh, PartitionSpec as P

HD = 128
GROUP = 4
KVH = 8
SPAN = 96
QTR = 24
NTOK = 6144
NSPAN = 64
NDOC = 8
TILE = 1536
HALF = TILE // 2
NTILE = -(-NTOK // TILE)
PIECE = QTR * GROUP
ROWS = 8 * PIECE
LANES = 256
NGROUP = ROWS // LANES
SCALE = HD**-0.5
LOG2E = 1.4426950408889634
NEG = -1e30

AXES = ("z", "xh", "c", "xl", "y")
PLANE = ("xh", "c", "xl", "y")

NT = (((1,), (1,)), ((), ()))
NN = (((1,), (0,)), ((), ()))


def dot(a, b, dims=NN):
    return lax.dot_general(a, b, dims, preferred_element_type=jnp.float32)


def doc_start(ends, place):
    start = jnp.zeros_like(place)
    for end in ends:
        start = jnp.where(end <= place, end, start)
    return start


def block_rows(order_ref, core, x, y, near, far, z):
    dx = jnp.where(core == 0, far, near)
    dy = jnp.where(core == 0, near, far)
    bx, by = (x - dx) & 3, (y - dy) & 3
    span = z * 8 + (bx >> 1) * 4 + core * 2 + (bx & 1)
    return pl.multiple_of(order_ref[span] * SPAN + by * QTR, 8)


def attention_kernel(where_ref, order_ref, lens_ref, *refs):
    in_refs, (qg_ref, outs_ref), refs = refs[:8], refs[8:10], refs[10:]
    out_refs, refs = refs[:8], refs[8:]
    (
        k_ref,
        v_ref,
        s_ref,
        p_ref,
        m_ref,
        acc_ref,
        dq_ref,
        turned_ref,
        dkt_ref,
        dvt_ref,
        dkv_ref,
        q_ref,
        g_ref,
        qpos_ref,
        blocks_ref,
        rows_ref,
        sems,
    ) = refs
    xh, c, xl, y = (where_ref[i] for i in range(4))
    x = xh * 2 + xl
    get_rows = pltpu.make_async_copy(qg_ref, rows_ref, sems.at[8])
    get_rows.start()
    get_blocks = [
        pltpu.make_async_copy(in_refs[i], blocks_ref.at[i], sems.at[i]) for i in range(8)
    ]
    for copy in get_blocks:
        copy.start()

    v_ref[:, HD:] = jnp.ones((NTOK, HD), jnp.bfloat16)
    for ref in (dkt_ref, dvt_ref, acc_ref, dq_ref):
        ref[...] = jnp.zeros_like(ref)
    m_ref[...] = jnp.full(m_ref.shape, NEG, jnp.float32)

    ends = []
    total_len = jnp.int32(0)
    for d in range(NDOC):
        total_len = total_len + lens_ref[d]
        ends.append(total_len)

    places = [
        order_ref[j * 8 + xh * 4 + c * 2 + xl] * SPAN + y * QTR for j in range(8)
    ]
    ranks = [sum((p < places[i]).astype(jnp.int32) for p in places) for i in range(8)]
    sorted_places = [
        sum(jnp.where(ranks[j] == i, places[j], 0) for j in range(8)) for i in range(8)
    ]

    get_rows.wait()
    row_ids = lax.broadcasted_iota(jnp.int32, (QTR, HD), 0)
    for pair in range(4):
        both = rows_ref[2 * pair * QTR : (2 * pair + 2) * QTR, :].astype(jnp.float32)
        for j in (2 * pair, 2 * pair + 1):
            qpos = places[j] + row_ids
            qstart = doc_start(ends, qpos)
            part = both[(j % 2) * QTR : (j % 2 + 1) * QTR]
            for h in range(GROUP):
                at = pl.ds(pl.multiple_of(ranks[j] * PIECE + h * QTR, 8), QTR)
                q_ref[at, :] = part[:, h * HD : (h + 1) * HD]
                g_ref[at, :] = part[:, (GROUP + h) * HD : (GROUP + h + 1) * HD]
                qpos_ref[0, at, :] = qpos
                qpos_ref[1, at, :] = qstart

    for i in range(8):
        core = 1 - c if i < 4 else c
        get_blocks[i].wait()

        def place_keys(zp, carry):
            for near in range(4):
                at = pl.multiple_of((near * 4 + zp) * 2 * QTR, 16)
                both = blocks_ref[i, pl.ds(at, 2 * QTR), :].astype(jnp.float32)
                for u in range(2):
                    first = block_rows(order_ref, core, x, y, near, i % 4, 2 * zp + u)
                    dkv_ref[pl.ds(first, QTR), :] = both[u * QTR : (u + 1) * QTR]
            return carry

        lax.fori_loop(0, 4, place_keys, 0, unroll=True)

    def round_keys(t, carry):
        first = pl.multiple_of(t * 512, 512)
        kv = dkv_ref[pl.ds(first, 512), :].astype(jnp.bfloat16)
        k_ref[pl.ds(first, 512), :] = kv[:, :HD]
        v_ref[pl.ds(first, 512), :HD] = kv[:, HD:]
        return carry

    lax.fori_loop(0, NTOK // 512, round_keys, 0)

    lane = lax.broadcasted_iota(jnp.int32, (LANES, HD), 1)
    groups = []
    for g in range(ROWS // LANES):
        low = doc_start(ends, sorted_places[g * LANES // PIECE])
        high = sorted_places[((g + 1) * LANES - 1) // PIECE] + QTR
        low = (low // HD) * HD
        groups.append((g, slice(g * LANES, (g + 1) * LANES), low, (high - low + HALF - 1) // HALF))

    def run(step, halves):
        def whole(t, carry):
            step(t, TILE)
            return carry

        lax.fori_loop(0, halves >> 1, whole, 0)

        @pl.when(halves % 2 == 1)
        def _():
            step(halves >> 1, HALF)

    for g, rows, low, halves in groups:
        q = q_ref[rows, :].astype(jnp.bfloat16)

        def score_step(t, size):
            first = pl.multiple_of(jnp.minimum(low + t * TILE, NTOK - size), HD)
            s = dot(q, k_ref[pl.ds(first, size), :], NT)
            qpos = qpos_ref[0, rows, :]
            qstart = jnp.maximum(qpos_ref[1, rows, :], low + t * TILE)
            top = m_ref[g]
            for j in range(size // HD):
                kpos = lane + (first + j * HD)
                seen = (kpos <= qpos) & (kpos >= qstart)
                part = jnp.where(seen, s[:, j * HD : (j + 1) * HD], NEG)
                s_ref[g, t, :, j * HD : (j + 1) * HD] = part
                top = jnp.maximum(top, part)
            m_ref[g] = top

        run(score_step, halves)

    m_ref[...] = jnp.broadcast_to(jnp.max(m_ref[...], axis=2, keepdims=True), m_ref.shape)

    for g, rows, low, halves in groups:

        def value_step(t, size):
            first = pl.multiple_of(jnp.minimum(low + t * TILE, NTOK - size), HD)
            top = m_ref[g]
            parts = [
                jnp.exp2((s_ref[g, t, :, j * HD : (j + 1) * HD] - top) * (SCALE * LOG2E))
                for j in range(size // HD)
            ]
            p = jnp.concatenate(parts, axis=1).astype(jnp.bfloat16)
            p_ref[g, t, :, :size] = p
            acc_ref[g] += dot(p, v_ref[pl.ds(first, size), :])

        run(value_step, halves)

    for g, rows, low, halves in groups:
        inv = 1.0 / acc_ref[g, :, HD:]
        attended = (acc_ref[g, :, :HD] * inv).astype(jnp.bfloat16).astype(jnp.float32)
        gs32 = g_ref[rows, :] * inv
        g_ref[rows, :] = gs32
        m_ref[g] = jnp.broadcast_to(
            jnp.sum(attended * gs32, axis=1, keepdims=True), (LANES, HD)
        )
        turned_ref[0, :, rows] = q_ref[rows, :].T.astype(jnp.bfloat16)
        turned_ref[1, :, rows] = gs32.T.astype(jnp.bfloat16)
        q_ref[rows, :] = attended

    for g, rows, low, halves in groups:
        gs = g_ref[rows, :].astype(jnp.bfloat16)
        qt, gst = turned_ref[0, :, rows], turned_ref[1, :, rows]
        grad_dot = m_ref[g]

        def grad_step(t, size):
            first = pl.multiple_of(jnp.minimum(low + t * TILE, NTOK - size), HD)
            p = p_ref[g, t, :, :size]
            dp = dot(gs, v_ref[pl.ds(first, size), :HD], NT)
            ds = jnp.concatenate(
                [
                    p[:, j * HD : (j + 1) * HD].astype(jnp.float32)
                    * (dp[:, j * HD : (j + 1) * HD] - grad_dot)
                    for j in range(size // HD)
                ],
                axis=1,
            ).astype(jnp.bfloat16)
            dvt_ref[:, pl.ds(first, size)] += dot(gst, p)
            dq_ref[g] += dot(ds, k_ref[pl.ds(first, size), :])
            dkt_ref[:, pl.ds(first, size)] += dot(qt, ds)

        run(grad_step, halves)

    for g, rows, low, halves in groups:
        g_ref[rows, :] = dq_ref[g] * SCALE

    for pair in range(4):
        for h in range(GROUP):
            spots = [
                pl.ds(pl.multiple_of(ranks[j] * PIECE + h * QTR, 8), QTR)
                for j in (2 * pair, 2 * pair + 1)
            ]
            at = slice(2 * pair * QTR, (2 * pair + 2) * QTR)
            rows_ref[at, h * HD : (h + 1) * HD] = jnp.concatenate(
                [q_ref[spot, :] for spot in spots], axis=0
            ).astype(jnp.bfloat16)
            rows_ref[at, (GROUP + h) * HD : (GROUP + h + 1) * HD] = jnp.concatenate(
                [g_ref[spot, :] for spot in spots], axis=0
            ).astype(jnp.bfloat16)
    put_rows = pltpu.make_async_copy(rows_ref, outs_ref, sems.at[8])
    put_rows.start()

    def turn(t, carry):
        first = pl.multiple_of(t * 2048, 2048)
        for ref, at, scale in ((dkt_ref, 0, SCALE), (dvt_ref, HD, 1.0)):
            part = ref[:, pl.ds(first, 2048)] * scale
            part = part.astype(jnp.bfloat16).T.astype(jnp.float32)
            dkv_ref[pl.ds(first, 2048), at : at + HD] = part
        return carry

    lax.fori_loop(0, NTOK // 2048, turn, 0)

    put_blocks = []
    for i in range(8):
        core = 1 - c if i < 4 else c

        def give_grads(zp, carry):
            for near in range(4):
                both = jnp.concatenate(
                    [
                        dkv_ref[
                            pl.ds(block_rows(order_ref, core, x, y, near, i % 4, 2 * zp + u), QTR),
                            :,
                        ]
                        for u in range(2)
                    ],
                    axis=0,
                )
                at = pl.multiple_of((near * 4 + zp) * 2 * QTR, 16)
                blocks_ref[i, pl.ds(at, 2 * QTR), :] = both.astype(jnp.bfloat16)
            return carry

        lax.fori_loop(0, 4, give_grads, 0, unroll=True)
        put_blocks.append(pltpu.make_async_copy(blocks_ref.at[i], out_refs[i], sems.at[i]))
        put_blocks[i].start()
    for copy in put_blocks:
        copy.wait()
    put_rows.wait()


def attention(where, order, lens, own, other, qg):
    smem = pl.BlockSpec(memory_space=pltpu.SMEM)
    anywhere = pl.BlockSpec(memory_space=pl.ANY)
    bf, f32 = jnp.bfloat16, jnp.float32
    flat = [b.reshape(-1, 2 * HD) for b in (*other, *own)]
    shape = own[0].shape
    block = jax.ShapeDtypeStruct(flat[0].shape, bf)
    rows = qg.reshape(-1, qg.shape[2])
    outs = pl.pallas_call(
        attention_kernel,
        out_shape=(jax.ShapeDtypeStruct(rows.shape, bf),) + (block,) * 8,
        in_specs=[smem] * 3 + [anywhere] * 9,
        out_specs=[anywhere] * 9,
        scratch_shapes=[
            pltpu.VMEM((NTOK, HD), bf),
            pltpu.VMEM((NTOK, 2 * HD), bf),
            pltpu.VMEM((NGROUP, NTILE, LANES, TILE), f32),
            pltpu.VMEM((NGROUP, NTILE, LANES, TILE), bf),
            pltpu.VMEM((NGROUP, LANES, HD), f32),
            pltpu.VMEM((NGROUP, LANES, 2 * HD), f32),
            pltpu.VMEM((NGROUP, LANES, HD), f32),
            pltpu.VMEM((2, HD, ROWS), bf),
            pltpu.VMEM((HD, NTOK), f32),
            pltpu.VMEM((HD, NTOK), f32),
            pltpu.VMEM((NTOK, 2 * HD), f32),
            pltpu.VMEM((ROWS, HD), f32),
            pltpu.VMEM((ROWS, HD), f32),
            pltpu.VMEM((2, ROWS, HD), jnp.int32),
            pltpu.VMEM((8, NTOK // 8, 2 * HD), bf),
            pltpu.VMEM((8 * QTR, 2 * GROUP * HD), bf),
            pltpu.SemaphoreType.DMA((9,)),
        ],
        compiler_params=pltpu.CompilerParams(vmem_limit_bytes=58 * 1024 * 1024),
        cost_estimate=pl.CostEstimate(
            flops=4 * 10**9, bytes_accessed=10**7, transcendentals=2 * 10**6
        ),
    )(where, order, lens, *flat, rows)
    grads = [b.reshape(shape) for b in outs[1:]]
    return outs[0].reshape(qg.shape), grads[4:], grads[:4]


def swap_cores(x):
    return lax.ppermute(x, "c", [(0, 1), (1, 0)])


def shift(x, steps, stage):
    pairs = []
    for c in range(2):
        for i in range(4):
            for y in range(4):
                if c == stage:
                    to = (i, (y + steps) % 4)
                else:
                    to = ((i + steps) % 4, y)
                at = lambda a, b: (((a // 2) * 2 + c) * 2 + a % 2) * 4 + b
                pairs.append((at(i, y), at(*to)))
    return lax.ppermute(x, PLANE, pairs)


def total(*parts):
    return sum(p.astype(jnp.float32) for p in parts).astype(jnp.bfloat16)


def per_device(query_rows, key_rows, value_rows, grad_output, span_order, doc_lengths):
    kv = jnp.concatenate(
        [key_rows.reshape(QTR, KVH, HD), value_rows.reshape(QTR, KVH, HD)], axis=2
    ).transpose(1, 0, 2)
    kv = lax.all_to_all(kv, "z", split_axis=0, concat_axis=0, tiled=True)
    qg = jnp.concatenate(
        [query_rows.reshape(QTR, KVH, -1), grad_output.reshape(QTR, KVH, -1)], axis=2
    ).transpose(1, 0, 2)
    qg = lax.all_to_all(qg, "z", split_axis=0, concat_axis=0, tiled=True)
    near = jnp.stack([kv] + [shift(kv, i, 0) for i in range(1, 4)])
    own = [near] + [shift(near, i, 1) for i in range(1, 4)]
    other = [swap_cores(b) for b in own]
    where = jnp.stack([lax.axis_index(a) for a in ("xh", "c", "xl", "y")]).astype(jnp.int32)
    outs, down, dother = attention(where, span_order, doc_lengths, own, other, qg)

    outs = lax.all_to_all(outs, "z", split_axis=0, concat_axis=0, tiled=True)
    dother = [swap_cores(b) for b in dother]
    far = [shift(total(down[i], dother[i]), 4 - i, 1) for i in range(1, 4)]
    near = total(down[0], dother[0], *far)
    dkv = total(near[0], *[shift(near[i], 4 - i, 0) for i in range(1, 4)])
    dkv = lax.all_to_all(dkv, "z", split_axis=0, concat_axis=0, tiled=True)
    half = GROUP * HD
    return (
        outs[:, :, :half].transpose(1, 0, 2).reshape(QTR, -1),
        outs[:, :, half:].transpose(1, 0, 2).reshape(QTR, -1),
        dkv[:, :, :HD].transpose(1, 0, 2).reshape(QTR, -1),
        dkv[:, :, HD:].transpose(1, 0, 2).reshape(QTR, -1),
    )


def solution(mesh):
    fine = Mesh(mesh.devices.reshape(8, 2, 2, 2, 4), AXES)
    rows = P(AXES, None)
    return jax.shard_map(
        per_device,
        mesh=fine,
        in_specs=(rows, rows, rows, rows, P(), P()),
        out_specs=(rows, rows, rows, rows),
        check_vma=False,
    )
```
